32 devices in a mesh: leaf: 4 (over z), front: 8 (over y, x, core).
Axes of the slice: x: 2, y: 2, z: 4, core: 2. Of those that a mesh axis runs over, the one named last changes fastest.
Arguments:
- stacked: float32 [8, 4096, 896], P('front', 'leaf'), may hold values from -2.34375 to 2.34375, as said below
- row_owner: int32 [8, 640, 1], P('front', 'leaf'), may hold values from 0 to 7; in each aligned block of 160 rows (0 to 159, 160 to 319, ..., all dimensions but the last counted through in order) at most 40 rows name the same one
- dest_local: int32 [8, 640], P('front', 'leaf'), may hold values from 0 to 63
Outputs:
- pivot_rows: float32 [8, 256, 896], P('front', 'leaf')
- assembled: float32 [8, 256, 640], P('front', 'leaf')
The draws below stay inside these ranges and needn't reach their ends.
Inputs may be any that keep to these rules, and one draw needn't show every extreme that they name: `stacked`: entries of a front's rows carry a scale of their row and one of their column. `row_owner`: among the 160 contribution rows of a front on one leaf index, no owner is named by more than 40 of them.
All inputs are finite; a program needn't handle non-finite values.
Results may differ from the reference program's by a relative error of at most 0.000076.
Values sent between devices are 32-bit elements; how exact they have to be, the bound alone decides.
A program may use at most 64 MiB of HBM per device.

```python
import math
import jax
import jax.numpy as jnp
import numpy as np
from jax import lax

PIV = 256
PR_DEV = 64
COLS = 896
CB = 640
CB_DEV = 160
CAP = 40
FRONT_ROWS = 4096
N_LEAF = 4
N_FRONT = 8


def draw_stacked(key, part):
    keys = jax.random.split(jax.random.fold_in(key, 11), 3)
    shape = (N_FRONT, FRONT_ROWS, COLS)
    base = jnp.clip(jax.random.normal(keys[0], shape, jnp.float32), -6.0, 6.0)
    row_scale = jnp.exp(jax.random.uniform(keys[1], (N_FRONT, FRONT_ROWS, 1), jnp.float32, 0.0, math.log(10.0)))
    col_scale = jnp.exp(jax.random.uniform(keys[2], (N_FRONT, 1, COLS), jnp.float32, 0.0, math.log(10.0)))
    return base * row_scale * col_scale * (0.25 / math.sqrt(FRONT_ROWS))


def plant(values, key, least, largest):
    shape = values.shape
    spot = [jax.random.randint(jax.random.fold_in(key, axis), (), 0, shape[axis]) for axis in range(len(shape))]
    values = values.at[tuple(spot)].set(least)
    longest = shape.index(max(shape))
    spot[longest] = (spot[longest] + 1) % shape[longest]
    return values.at[tuple(spot)].set(largest)


def shared_out(own_key, own, number, rows, count, top, limit, lean):
    order = jax.random.permutation(own_key, count)
    crowded, common = shares(count, rows * top, limit, lean, True), shares(count, rows * top, limit, lean, False)
    places = jnp.arange(count)

    def named(lengths, offset_by):
        used = int((lengths > 0).sum())
        fixed = max(1, used // 4)
        shifted = fixed + (places - fixed + offset_by * (used - fixed)) % max(1, count - fixed)
        return jnp.zeros((count,), jnp.int32).at[order[jnp.where(places < fixed, places, shifted)]].set(jnp.asarray(lengths, jnp.int32))

    lengths = jnp.where(number % 4 == 0, named(crowded, number // 4), named(common, number - number // 4 - 1))
    mixed = jax.random.permutation(jax.random.fold_in(own, 3), count)
    giver, receiver = mixed[0:count // 2 * 2:2], mixed[1:count // 2 * 2:2]
    margin = jnp.minimum(lengths[giver] - 1, limit - lengths[receiver]) // 2
    margin = jnp.where((giver == order[0]) | (receiver == order[0]) | (lengths[receiver] == 0), 0, jnp.maximum(margin, 0))
    shifted = jax.random.randint(jax.random.fold_in(own, 4), (count // 2,), 0, 1 << 20) % (margin + 1)
    lengths = lengths.at[giver].add(-shifted).at[receiver].add(shifted)
    members = jnp.searchsorted(jnp.cumsum(lengths), jnp.arange(rows * top), side="right").astype(jnp.int32)
    table = members.reshape(top, rows).T
    table = table[jax.random.permutation(jax.random.fold_in(own, 1), rows)]
    offset_by = jax.random.randint(jax.random.fold_in(own, 2), (rows, 1), 0, top)
    return jnp.take_along_axis(table, (jnp.arange(top)[None, :] + offset_by) % top, axis=1)


def shares(number_of, total, limit, slope, full):
    loads = [(1 << 20) // math.isqrt(standing ** slope) + 1 for standing in range(1, number_of + 1)]
    largest = limit if full else min(limit, max(-(-total // number_of), total * loads[0] // sum(loads)))
    least = 1 if total - largest >= number_of - 1 else 0
    counts, spare = [largest] + [least] * (number_of - 1), total - largest - least * (number_of - 1)
    while spare > 0:
        candidates = [i for i in range(1, number_of) if counts[i] < largest] or [i for i in range(1, number_of) if counts[i] < limit]
        pool, remaining = sum([loads[i] for i in candidates]), spare
        for i in candidates:
            more = min(limit - counts[i], max(1, remaining * loads[i] // pool), spare)
            counts[i] = counts[i] + more
            spare = spare - more
    return np.array(counts)


def setup_inputs(seed: int = 0) -> dict:
    splits = jax.random.split(jax.random.key(seed), 4)
    stacked = draw_stacked(jax.random.fold_in(splits[3], 71), 0)
    row_owner_keys = jax.random.split(jax.random.fold_in(splits[1], 1), N_FRONT * CB // CB_DEV)
    row_owner_turns = jax.random.permutation(jax.random.fold_in(splits[1], 3), N_FRONT * CB // CB_DEV)
    row_owner = jax.vmap(lambda own, number: shared_out(jax.random.fold_in(splits[1], 2), own, number, CB_DEV, N_FRONT, 1, CAP, 2))(row_owner_keys, row_owner_turns).reshape((N_FRONT, CB, 1))
    dest_local = plant(jax.random.randint(splits[2], (N_FRONT, CB), 0, PR_DEV), jax.random.fold_in(splits[2], 1), 0, PR_DEV - 1).astype(jnp.int32)
    return {"stacked": stacked, "row_owner": row_owner, "dest_local": dest_local}


highest = lax.Precision.HIGHEST

def front_factor(front_rows):
    gram_front = lax.dot_general(front_rows.astype(jnp.float32), front_rows.astype(jnp.float32), (((0,), (0,)), ((), ())), precision=highest, preferred_element_type=jnp.float32)
    return jnp.linalg.cholesky(gram_front).T

def reference(stacked, row_owner, dest_local):
    factors = lax.map(front_factor, stacked)
    pivots = factors[:, :PIV, :]
    contribution = factors[:, PIV:, PIV:]
    width = contribution.shape[2]
    leaf_of_row = (jnp.arange(width).astype(jnp.int32) // CB_DEV).astype(jnp.int32)
    target = row_owner[:, :, 0].astype(jnp.int32) * (N_LEAF * PR_DEV) + leaf_of_row[None, :] * PR_DEV + dest_local.astype(jnp.int32)
    flat_rows = contribution.reshape(-1, width)
    summed = jnp.zeros((N_FRONT * N_LEAF * PR_DEV, width), jnp.float32).at[target.reshape(-1)].add(flat_rows)
    return (pivots, summed.reshape(N_FRONT, N_LEAF * PR_DEV, width))
```

```python
import functools
import jax
import jax.numpy as jnp
from jax import lax
from jax.experimental import pallas as pl
from jax.experimental.pallas import tpu as pltpu
from jax.sharding import PartitionSpec as P

PIV = 256
PR_DEV = 64
STRIP = 8
SUB = 32
PANEL = 128


highest = lax.Precision.HIGHEST


def factor_strip(a_ref, start, panel, strip, width):
    blocks = width // PANEL
    diag = a_ref[pl.ds(start, STRIP), pl.ds(pl.multiple_of(panel * PANEL, PANEL), PANEL)]
    c = {}
    for k in range(STRIP):
        lane = strip * STRIP + k
        column = jnp.broadcast_to(diag[:, lane:lane + 1], (STRIP, PANEL))
        for i in range(k, STRIP):
            c[i, k] = jnp.broadcast_to(column[i:i + 1, :], (STRIP, PANEL))
    body = [a_ref[pl.ds(start, STRIP), b * PANEL:(b + 1) * PANEL] for b in range(blocks)]
    body.append(diag)
    rows = [[jnp.broadcast_to(x[k:k + 1, :], (STRIP, PANEL)) for x in body] for k in range(STRIP)]
    for k in range(STRIP):
        inv = lax.rsqrt(c[k, k])
        rows[k] = [x * inv for x in rows[k]]
        for i in range(k + 1, STRIP):
            c[i, k] = c[i, k] * inv
        for i in range(k + 1, STRIP):
            for j in range(k + 1, i + 1):
                c[i, j] = c[i, j] - c[i, k] * c[j, k]
            rows[i] = [x - c[i, k] * y for x, y in zip(rows[i], rows[k])]
    sub = lax.broadcasted_iota(jnp.int32, (STRIP, PANEL), 0)
    lanes = lax.broadcasted_iota(jnp.int32, (STRIP, PANEL), 1)
    for b in range(blocks):
        out = rows[0][b]
        for k in range(1, STRIP):
            out = jnp.where(sub == k, rows[k][b], out)
        a_ref[pl.ds(start, STRIP), b * PANEL:(b + 1) * PANEL] = out
    return rows, sub, lanes


def cholesky_kernel(g_ref, a_ref):
    width = a_ref.shape[0]
    blocks = width // PANEL
    a_ref[...] = g_ref[...]

    def one_panel(panel, carry):
        base = pl.multiple_of(panel * PANEL, PANEL)
        for group in range(PANEL // SUB):
            for t in range(SUB // STRIP):
                strip = group * (SUB // STRIP) + t
                start = pl.multiple_of(base + strip * STRIP, STRIP)
                rows, sub, lanes = factor_strip(a_ref, start, panel, strip, width)
                for later in range(strip + 1, (group + 1) * (SUB // STRIP)):
                    below = pl.multiple_of(base + later * STRIP, STRIP)
                    picked = lanes == sub + later * STRIP
                    mult = [
                        jnp.sum(jnp.where(picked, rows[k][blocks], 0.0), axis=1, keepdims=True)
                        for k in range(STRIP)
                    ]
                    for b in range(blocks):
                        at = (pl.ds(below, STRIP), slice(b * PANEL, (b + 1) * PANEL))
                        terms = [mult[k] * rows[k][b] for k in range(STRIP)]
                        while len(terms) > 1:
                            terms = [x + y for x, y in zip(terms[::2], terms[1::2])]
                        a_ref[at] = a_ref[at] - terms[0]
            if group < PANEL // SUB - 1:
                done = pl.ds(pl.multiple_of(base + group * SUB, SUB), SUB)
                left = PANEL - (group + 1) * SUB
                head = a_ref[done, pl.ds(base, PANEL)].T[(group + 1) * SUB:, :]
                rest = pl.ds(pl.multiple_of(base + (group + 1) * SUB, SUB), left)
                a_ref[rest, :] = a_ref[rest, :] - jnp.dot(
                    head, a_ref[done, :], precision=highest, preferred_element_type=jnp.float32
                )

        def trailing(j, carry):
            rest = pl.ds(pl.multiple_of(j * PANEL, PANEL), PANEL)
            head = a_ref[pl.ds(base, PANEL), rest].T
            a_ref[rest, :] = a_ref[rest, :] - jnp.dot(
                head, a_ref[pl.ds(base, PANEL), :], precision=highest, preferred_element_type=jnp.float32
            )
            return carry

        lax.fori_loop(panel + 1, blocks, trailing, 0)
        return carry

    lax.fori_loop(0, blocks, one_panel, 0)
    for r in range(blocks):
        rows = slice(r * PANEL, (r + 1) * PANEL)
        if r:
            a_ref[rows, :r * PANEL] = jnp.zeros((PANEL, r * PANEL), jnp.float32)
        upper = lax.broadcasted_iota(jnp.int32, (PANEL, PANEL), 0) <= lax.broadcasted_iota(
            jnp.int32, (PANEL, PANEL), 1
        )
        a_ref[rows, rows] = jnp.where(upper, a_ref[rows, rows], 0.0)


def cholesky_upper(gram):
    return pl.pallas_call(
        cholesky_kernel,
        out_shape=jax.ShapeDtypeStruct(gram.shape, jnp.float32),
        in_specs=[pl.BlockSpec(memory_space=pltpu.VMEM)],
        out_specs=pl.BlockSpec(memory_space=pltpu.VMEM),
        compiler_params=pltpu.CompilerParams(vmem_limit_bytes=40 * 1024 * 1024),
        name="cholesky_upper",
    )(gram)


def shards(stacked, row_owner, dest_local):
    local_rows = stacked[0]
    columns = local_rows.shape[1]
    gram_local = lax.dot_general(
        local_rows,
        local_rows,
        (((0,), (0,)), ((), ())),
        precision=highest,
        preferred_element_type=jnp.float32,
    )
    gram_total = lax.psum(gram_local, "leaf")
    upper_factor = cholesky_upper(gram_total)
    leaf_index = lax.axis_index("leaf")
    pivot_count = PIV // lax.axis_size("leaf")
    pivot_part = lax.dynamic_slice_in_dim(upper_factor, leaf_index * pivot_count, pivot_count, 0)
    contrib_count = row_owner.shape[1]
    contrib_width = columns - PIV
    block_rows = lax.dynamic_slice_in_dim(
        upper_factor, PIV + leaf_index * contrib_count, contrib_count, 0
    )[:, PIV:]
    owners = row_owner[0, :, 0]
    targets = dest_local[0]
    fronts = lax.axis_size("front")
    capacity = max(2, (2 * contrib_count + fronts - 1) // fronts)
    same_owner = owners[:, None] == owners[None, :]
    earlier = lax.broadcasted_iota(
        jnp.int32, (contrib_count, contrib_count), 1
    ) < lax.broadcasted_iota(jnp.int32, (contrib_count, contrib_count), 0)
    slot_rank = jnp.sum((same_owner & earlier).astype(jnp.int32), axis=1)
    slot_index = owners * capacity + slot_rank
    select = (
        slot_index[None, :]
        == lax.broadcasted_iota(jnp.int32, (fronts * capacity, contrib_count), 0)
    ).astype(jnp.float32)
    send_rows = jnp.dot(
        select, block_rows, precision=highest, preferred_element_type=jnp.float32
    ).reshape(fronts, capacity, contrib_width)
    send_dest = jnp.dot(
        select,
        (targets + 1).astype(jnp.float32),
        precision=highest,
        preferred_element_type=jnp.float32,
    ).reshape(fronts, capacity)
    got_rows, got_dest = (
        lax.all_to_all(send_rows, "front", split_axis=0, concat_axis=0, tiled=True),
        lax.all_to_all(send_dest, "front", split_axis=0, concat_axis=0, tiled=True),
    )
    place = (
        got_dest.reshape(1, -1) == lax.broadcasted_iota(jnp.float32, (PR_DEV, 1), 0) + 1.0
    ).astype(jnp.float32)
    assembled = jnp.dot(
        place,
        got_rows.reshape(-1, contrib_width),
        precision=highest,
        preferred_element_type=jnp.float32,
    )
    return (pivot_part[None], assembled[None])


def solution(mesh):
    return jax.shard_map(
        shards,
        mesh=mesh,
        in_specs=(P("front", "leaf", None), P("front", "leaf", None), P("front", "leaf")),
        out_specs=(P("front", "leaf", None), P("front", "leaf", None)),
        check_vma=False,
    )
```

```python
import functools
import jax
import jax.numpy as jnp
from jax import lax
from jax.experimental import pallas as pl
from jax.experimental.pallas import tpu as pltpu
from jax.sharding import PartitionSpec as P

PIV = 256
PR_DEV = 64
STRIP = 8
SUB = 32
PANEL = 128
CHUNK = 32
MESH = pl.DeviceIdType.MESH


highest = lax.Precision.HIGHEST


def factor_strip(a_ref, start, panel, strip, width):
    blocks = width // PANEL
    diag = a_ref[pl.ds(start, STRIP), pl.ds(pl.multiple_of(panel * PANEL, PANEL), PANEL)]
    c = {}
    for k in range(STRIP):
        lane = strip * STRIP + k
        column = jnp.broadcast_to(diag[:, lane:lane + 1], (STRIP, PANEL))
        for i in range(k, STRIP):
            c[i, k] = jnp.broadcast_to(column[i:i + 1, :], (STRIP, PANEL))
    body = [a_ref[pl.ds(start, STRIP), b * PANEL:(b + 1) * PANEL] for b in range(blocks)]
    body.append(diag)
    rows = [[jnp.broadcast_to(x[k:k + 1, :], (STRIP, PANEL)) for x in body] for k in range(STRIP)]
    for k in range(STRIP):
        inv = lax.rsqrt(c[k, k])
        rows[k] = [x * inv for x in rows[k]]
        for i in range(k + 1, STRIP):
            c[i, k] = c[i, k] * inv
        for i in range(k + 1, STRIP):
            for j in range(k + 1, i + 1):
                c[i, j] = c[i, j] - c[i, k] * c[j, k]
            rows[i] = [x - c[i, k] * y for x, y in zip(rows[i], rows[k])]
    sub = lax.broadcasted_iota(jnp.int32, (STRIP, PANEL), 0)
    lanes = lax.broadcasted_iota(jnp.int32, (STRIP, PANEL), 1)
    for b in range(blocks):
        out = rows[0][b]
        for k in range(1, STRIP):
            out = jnp.where(sub == k, rows[k][b], out)
        a_ref[pl.ds(start, STRIP), b * PANEL:(b + 1) * PANEL] = out
    return rows, sub, lanes


def front_kernel(x_ref, a_ref, high, low, own, in_l, in_r, out_l, out_r, send_l, recv_l, send_r, recv_r):
    width = a_ref.shape[0]
    blocks = width // PANEL
    packed = (blocks + 1) // 2
    chunks = packed * PANEL // CHUNK
    per_panel = PANEL // CHUNK
    me, n = lax.axis_index("leaf"), lax.axis_size("leaf")
    has_left, has_right = me > 0, me < n - 1

    barrier = pltpu.get_barrier_semaphore()

    @pl.when(has_left)
    def _():
        pl.semaphore_signal(barrier, inc=1, device_id={"leaf": me - 1}, device_id_type=MESH)

    @pl.when(has_right)
    def _():
        pl.semaphore_signal(barrier, inc=1, device_id={"leaf": me + 1}, device_id_type=MESH)

    @pl.when(jnp.logical_not(has_left))
    def _():
        in_l[...] = jnp.zeros_like(in_l)

    @pl.when(jnp.logical_not(has_right))
    def _():
        in_r[...] = jnp.zeros_like(in_r)

    a_ref[...] = jnp.zeros_like(a_ref)
    high[...] = x_ref[...].astype(jnp.bfloat16)
    low[...] = (x_ref[...] - high[...].astype(jnp.float32)).astype(jnp.bfloat16)

    inner = jnp.logical_and(has_left, has_right)

    @pl.when(inner)
    def _():
        pl.semaphore_wait(barrier, 2)

    @pl.when(jnp.logical_not(inner))
    def _():
        pl.semaphore_wait(barrier, 1)

    def rows_of(c):
        return pl.ds(pl.multiple_of(c * CHUNK, CHUNK), CHUNK)

    def to_right(src, c):
        return pltpu.make_async_remote_copy(
            src_ref=src.at[rows_of(c)], dst_ref=in_l.at[rows_of(c)],
            send_sem=send_r.at[c], recv_sem=recv_l.at[c],
            device_id={"leaf": me + 1}, device_id_type=MESH,
        )

    def to_left(src, c):
        return pltpu.make_async_remote_copy(
            src_ref=src.at[rows_of(c)], dst_ref=in_r.at[rows_of(c)],
            send_sem=send_l.at[c], recv_sem=recv_r.at[c],
            device_id={"leaf": me - 1}, device_id_type=MESH,
        )

    def from_left(c):
        @pl.when(has_left)
        def _():
            to_right(out_r, c).wait_recv()

            @pl.when(has_right)
            def _():
                out_r[rows_of(c), :] = own[rows_of(c), :] + in_l[rows_of(c), :]
                to_right(out_r, c).start()

    def from_right(c):
        @pl.when(has_right)
        def _():
            to_left(out_l, c).wait_recv()

            @pl.when(has_left)
            def _():
                out_l[rows_of(c), :] = own[rows_of(c), :] + in_r[rows_of(c), :]
                to_left(out_l, c).start()

    first_half = 2 * me < n

    def near(c):
        @pl.when(first_half)
        def _():
            from_left(c)

        @pl.when(jnp.logical_not(first_half))
        def _():
            from_right(c)

    def far(c):
        @pl.when(first_half)
        def _():
            from_right(c)

        @pl.when(jnp.logical_not(first_half))
        def _():
            from_left(c)

    def gram(panel, rows, at):
        cols = slice(panel * PANEL, (panel + 1) * PANEL)
        xt = x_ref[:, cols].T
        ht = xt.astype(jnp.bfloat16)
        lt = (xt - ht.astype(jnp.float32)).astype(jnp.bfloat16)
        right = slice(panel * PANEL, width)
        own[rows, at] = (
            jnp.dot(ht, high[:, right], preferred_element_type=jnp.float32)
            + jnp.dot(ht, low[:, right], preferred_element_type=jnp.float32)
            + jnp.dot(lt, high[:, right], preferred_element_type=jnp.float32)
        )

    for q in range(packed):
        rows = slice(q * PANEL, (q + 1) * PANEL)
        gram(q, rows, slice(q * PANEL, width))
        if q:
            gram(blocks - q, rows, slice(0, q * PANEL))

        @pl.when(jnp.logical_not(has_left))
        def _():
            for c in range(q * per_panel, (q + 1) * per_panel):
                to_right(own, c).start()

        @pl.when(jnp.logical_not(has_right))
        def _():
            for c in range(q * per_panel, (q + 1) * per_panel):
                to_left(own, c).start()

        if q == 1:
            near(0)
        if q == 2:
            near(1)
            far(0)
    for c in range(2, per_panel + 1):
        near(c)
        far(c - 1)

    def one_panel(panel, carry):
        base = pl.multiple_of(panel * PANEL, PANEL)
        folded = panel >= packed
        source = pl.ds(pl.multiple_of(jnp.where(folded, blocks - panel, panel) * PANEL, PANEL), PANEL)
        shift = jnp.where(folded, panel, 0)

        def total(j, carry):
            at = pl.ds(pl.multiple_of((j - shift) * PANEL, PANEL), PANEL)
            a_ref[pl.ds(base, PANEL), pl.ds(pl.multiple_of(j * PANEL, PANEL), PANEL)] = (
                own[source, at] + in_l[source, at] + in_r[source, at]
            )
            return carry

        lax.fori_loop(panel, blocks, total, 0)

        def earlier(q, carry):
            done = pl.ds(pl.multiple_of(q * PANEL, PANEL), PANEL)
            head = a_ref[done, pl.ds(base, PANEL)].T
            a_ref[pl.ds(base, PANEL), :] = a_ref[pl.ds(base, PANEL), :] - jnp.dot(
                head, a_ref[done, :], precision=highest, preferred_element_type=jnp.float32
            )
            return carry

        lax.fori_loop(0, panel, earlier, 0)
        for group in range(PANEL // SUB):
            for part in range(SUB // CHUNK):
                c = (panel + 1) * per_panel + group * (SUB // CHUNK) + part

                @pl.when(c + 1 < chunks)
                def _():
                    near(c + 1)

                @pl.when(c < chunks)
                def _():
                    far(c)

            for t in range(SUB // STRIP):
                strip = group * (SUB // STRIP) + t
                start = pl.multiple_of(base + strip * STRIP, STRIP)
                rows, sub, lanes = factor_strip(a_ref, start, panel, strip, width)
                for later in range(strip + 1, (group + 1) * (SUB // STRIP)):
                    below = pl.multiple_of(base + later * STRIP, STRIP)
                    picked = lanes == sub + later * STRIP
                    mult = [
                        jnp.sum(jnp.where(picked, rows[k][blocks], 0.0), axis=1, keepdims=True)
                        for k in range(STRIP)
                    ]
                    for b in range(blocks):
                        at = (pl.ds(below, STRIP), slice(b * PANEL, (b + 1) * PANEL))
                        terms = [mult[k] * rows[k][b] for k in range(STRIP)]
                        while len(terms) > 1:
                            terms = [x + y for x, y in zip(terms[::2], terms[1::2])]
                        a_ref[at] = a_ref[at] - terms[0]
            if group < PANEL // SUB - 1:
                done = pl.ds(pl.multiple_of(base + group * SUB, SUB), SUB)
                left = PANEL - (group + 1) * SUB
                head = a_ref[done, pl.ds(base, PANEL)].T[(group + 1) * SUB:, :]
                rest = pl.ds(pl.multiple_of(base + (group + 1) * SUB, SUB), left)
                a_ref[rest, :] = a_ref[rest, :] - jnp.dot(
                    head, a_ref[done, :], precision=highest, preferred_element_type=jnp.float32
                )
        upper = lax.broadcasted_iota(jnp.int32, (PANEL, PANEL), 0) <= lax.broadcasted_iota(
            jnp.int32, (PANEL, PANEL), 1
        )
        at = (pl.ds(base, PANEL), pl.ds(base, PANEL))
        a_ref[at] = jnp.where(upper, a_ref[at], 0.0)
        return carry

    lax.fori_loop(0, blocks, one_panel, 0)
    for r in range(1, blocks):
        a_ref[r * PANEL:(r + 1) * PANEL, :r * PANEL] = jnp.zeros((PANEL, r * PANEL), jnp.float32)

    def finish(c, carry):
        @pl.when(has_right)
        def _():
            to_right(out_r, c).wait_send()

        @pl.when(has_left)
        def _():
            to_left(out_l, c).wait_send()

        return carry

    lax.fori_loop(0, chunks, finish, 0)


def front_factor(x):
    rows, width = x.shape
    packed = (width // PANEL + 1) // 2 * PANEL
    sums = pltpu.VMEM((packed, width), jnp.float32)
    sems = pltpu.SemaphoreType.DMA((packed // CHUNK,))
    return pl.pallas_call(
        front_kernel,
        out_shape=jax.ShapeDtypeStruct((width, width), jnp.float32),
        in_specs=[pl.BlockSpec(memory_space=pltpu.VMEM)],
        out_specs=pl.BlockSpec(memory_space=pltpu.VMEM),
        scratch_shapes=[pltpu.VMEM((rows, width), jnp.bfloat16)] * 2 + [sums] * 5 + [sems] * 4,
        compiler_params=pltpu.CompilerParams(
            vmem_limit_bytes=48 * 1024 * 1024, collective_id=0, has_side_effects=True
        ),
        name="front_factor",
    )(x)


def shards(stacked, row_owner, dest_local):
    local_rows = stacked[0]
    columns = local_rows.shape[1]
    upper_factor = front_factor(local_rows)
    leaf_index = lax.axis_index("leaf")
    pivot_count = PIV // lax.axis_size("leaf")
    pivot_part = lax.dynamic_slice_in_dim(upper_factor, leaf_index * pivot_count, pivot_count, 0)
    contrib_count = row_owner.shape[1]
    contrib_width = columns - PIV
    block_rows = lax.dynamic_slice_in_dim(
        upper_factor, PIV + leaf_index * contrib_count, contrib_count, 0
    )[:, PIV:]
    owners = row_owner[0, :, 0]
    targets = dest_local[0]
    fronts = lax.axis_size("front")
    capacity = max(2, (2 * contrib_count + fronts - 1) // fronts)
    same_owner = owners[:, None] == owners[None, :]
    earlier = lax.broadcasted_iota(
        jnp.int32, (contrib_count, contrib_count), 1
    ) < lax.broadcasted_iota(jnp.int32, (contrib_count, contrib_count), 0)
    slot_rank = jnp.sum((same_owner & earlier).astype(jnp.int32), axis=1)
    slot_index = owners * capacity + slot_rank
    select = (
        slot_index[None, :]
        == lax.broadcasted_iota(jnp.int32, (fronts * capacity, contrib_count), 0)
    ).astype(jnp.float32)
    send_rows = jnp.dot(
        select, block_rows, precision=highest, preferred_element_type=jnp.float32
    ).reshape(fronts, capacity, contrib_width)
    send_dest = jnp.dot(
        select,
        (targets + 1).astype(jnp.float32),
        precision=highest,
        preferred_element_type=jnp.float32,
    ).reshape(fronts, capacity)
    got_rows, got_dest = (
        lax.all_to_all(send_rows, "front", split_axis=0, concat_axis=0, tiled=True),
        lax.all_to_all(send_dest, "front", split_axis=0, concat_axis=0, tiled=True),
    )
    place = (
        got_dest.reshape(1, -1) == lax.broadcasted_iota(jnp.float32, (PR_DEV, 1), 0) + 1.0
    ).astype(jnp.float32)
    assembled = jnp.dot(
        place,
        got_rows.reshape(-1, contrib_width),
        precision=highest,
        preferred_element_type=jnp.float32,
    )
    return (pivot_part[None], assembled[None])


def solution(mesh):
    return jax.shard_map(
        shards,
        mesh=mesh,
        in_specs=(P("front", "leaf", None), P("front", "leaf", None), P("front", "leaf")),
        out_specs=(P("front", "leaf", None), P("front", "leaf", None)),
        check_vma=False,
    )
```

```python
import functools
import jax
import jax.numpy as jnp
from jax import lax
from jax.experimental import pallas as pl
from jax.experimental.pallas import tpu as pltpu
from jax.sharding import PartitionSpec as P

PIV = 256
PR_DEV = 64
STRIP = 8
SUB = 32
PANEL = 128
CHUNK = 32
MESH = pl.DeviceIdType.MESH


highest = lax.Precision.HIGHEST


def factor_strip(a_ref, start, panel, strip, width):
    blocks = width // PANEL
    diag = a_ref[pl.ds(start, STRIP), pl.ds(pl.multiple_of(panel * PANEL, PANEL), PANEL)]
    c = {}
    for k in range(STRIP):
        lane = strip * STRIP + k
        column = jnp.broadcast_to(diag[:, lane:lane + 1], (STRIP, PANEL))
        for i in range(k, STRIP):
            c[i, k] = jnp.broadcast_to(column[i:i + 1, :], (STRIP, PANEL))
    body = [a_ref[pl.ds(start, STRIP), b * PANEL:(b + 1) * PANEL] for b in range(blocks)]
    body.append(diag)
    rows = [[jnp.broadcast_to(x[k:k + 1, :], (STRIP, PANEL)) for x in body] for k in range(STRIP)]
    for k in range(STRIP):
        inv = lax.rsqrt(c[k, k])
        rows[k] = [x * inv for x in rows[k]]
        for i in range(k + 1, STRIP):
            c[i, k] = c[i, k] * inv
        for i in range(k + 1, STRIP):
            for j in range(k + 1, i + 1):
                c[i, j] = c[i, j] - c[i, k] * c[j, k]
            rows[i] = [x - c[i, k] * y for x, y in zip(rows[i], rows[k])]
    sub = lax.broadcasted_iota(jnp.int32, (STRIP, PANEL), 0)
    lanes = lax.broadcasted_iota(jnp.int32, (STRIP, PANEL), 1)
    for b in range(blocks):
        out = rows[0][b]
        for k in range(1, STRIP):
            out = jnp.where(sub == k, rows[k][b], out)
        a_ref[pl.ds(start, STRIP), b * PANEL:(b + 1) * PANEL] = out
    return rows, sub, lanes


def front_kernel(
    x_ref, select_ref, dest_ref, pivot_ref, sum_ref, a_ref, high, low, own, in_l, in_r, out_l, out_r,
    rows_out, rows_in, dest_in, send_l, recv_l, send_r, recv_r, row_send, row_recv, dest_send, dest_recv,
):
    width = a_ref.shape[0]
    blocks = width // PANEL
    packed = (blocks + 1) // 2
    chunks = packed * PANEL // CHUNK
    per_panel = PANEL // CHUNK
    me, n = lax.axis_index("leaf"), lax.axis_size("leaf")
    has_left, has_right = me > 0, me < n - 1
    front, fronts = lax.axis_index("front"), lax.axis_size("front")
    slots, contrib_count = select_ref.shape
    capacity = slots // fronts
    contrib_blocks = (width - PIV) // PANEL
    first_block = me * contrib_count // PANEL
    last_panel = (PIV + (me + 1) * contrib_count - 1) // PANEL
    peers = [lax.rem(front + d, fronts) for d in range(1, fronts)]

    barrier = pltpu.get_barrier_semaphore()

    @pl.when(has_left)
    def _():
        pl.semaphore_signal(barrier, inc=1, device_id={"leaf": me - 1}, device_id_type=MESH)

    @pl.when(has_right)
    def _():
        pl.semaphore_signal(barrier, inc=1, device_id={"leaf": me + 1}, device_id_type=MESH)

    rows_in[...] = jnp.zeros_like(rows_in)
    for peer in peers:
        pl.semaphore_signal(barrier, inc=1, device_id={"front": peer}, device_id_type=MESH)

    @pl.when(jnp.logical_not(has_left))
    def _():
        in_l[...] = jnp.zeros_like(in_l)

    @pl.when(jnp.logical_not(has_right))
    def _():
        in_r[...] = jnp.zeros_like(in_r)

    a_ref[...] = jnp.zeros_like(a_ref)
    high[...] = x_ref[...].astype(jnp.bfloat16)
    low[...] = (x_ref[...] - high[...].astype(jnp.float32)).astype(jnp.bfloat16)

    inner = jnp.logical_and(has_left, has_right)

    @pl.when(inner)
    def _():
        pl.semaphore_wait(barrier, 2 + fronts - 1)

    @pl.when(jnp.logical_not(inner))
    def _():
        pl.semaphore_wait(barrier, 1 + fronts - 1)

    def slots_of(g):
        return pl.ds(pl.multiple_of(g * capacity, STRIP), capacity)

    def dest_copy(to, src):
        return pltpu.make_async_remote_copy(
            src_ref=dest_ref.at[slots_of(to)], dst_ref=dest_in.at[slots_of(src)],
            send_sem=dest_send.at[to], recv_sem=dest_recv.at[src],
            device_id={"front": to}, device_id_type=MESH,
        )

    def row_copy(to, src, j):
        at = pl.ds(pl.multiple_of(j * PANEL, PANEL), PANEL)
        return pltpu.make_async_remote_copy(
            src_ref=rows_out.at[slots_of(to), at], dst_ref=rows_in.at[slots_of(src), at],
            send_sem=row_send.at[to, j], recv_sem=row_recv.at[src, j],
            device_id={"front": to}, device_id_type=MESH,
        )

    def send_rows():
        start = pl.multiple_of(PIV + me * contrib_count, STRIP)
        shape = (contrib_count, width - PIV)
        row = lax.broadcasted_iota(jnp.int32, shape, 0) + me * contrib_count
        rows = jnp.where(
            row <= lax.broadcasted_iota(jnp.int32, shape, 1), a_ref[pl.ds(start, contrib_count), PIV:], 0.0
        )
        rows_out[...] = jnp.dot(
            select_ref[...], rows, precision=highest, preferred_element_type=jnp.float32
        )
        for peer in peers:
            def one(j, carry, peer=peer):
                row_copy(peer, front, j).start()
                return carry

            lax.fori_loop(first_block, contrib_blocks, one, 0)
        rows_in[slots_of(front), :] = rows_out[slots_of(front), :]

    def rows_of(c):
        return pl.ds(pl.multiple_of(c * CHUNK, CHUNK), CHUNK)

    def to_right(src, c):
        return pltpu.make_async_remote_copy(
            src_ref=src.at[rows_of(c)], dst_ref=in_l.at[rows_of(c)],
            send_sem=send_r.at[c], recv_sem=recv_l.at[c],
            device_id={"leaf": me + 1}, device_id_type=MESH,
        )

    def to_left(src, c):
        return pltpu.make_async_remote_copy(
            src_ref=src.at[rows_of(c)], dst_ref=in_r.at[rows_of(c)],
            send_sem=send_l.at[c], recv_sem=recv_r.at[c],
            device_id={"leaf": me - 1}, device_id_type=MESH,
        )

    def from_left(c):
        @pl.when(has_left)
        def _():
            to_right(out_r, c).wait_recv()

            @pl.when(has_right)
            def _():
                out_r[rows_of(c), :] = own[rows_of(c), :] + in_l[rows_of(c), :]
                to_right(out_r, c).start()

    def from_right(c):
        @pl.when(has_right)
        def _():
            to_left(out_l, c).wait_recv()

            @pl.when(has_left)
            def _():
                out_l[rows_of(c), :] = own[rows_of(c), :] + in_r[rows_of(c), :]
                to_left(out_l, c).start()

    first_half = 2 * me < n

    def near(c):
        @pl.when(first_half)
        def _():
            from_left(c)

        @pl.when(jnp.logical_not(first_half))
        def _():
            from_right(c)

    def far(c):
        @pl.when(first_half)
        def _():
            from_right(c)

        @pl.when(jnp.logical_not(first_half))
        def _():
            from_left(c)

    def gram(panel, rows, at):
        cols = slice(panel * PANEL, (panel + 1) * PANEL)
        xt = x_ref[:, cols].T
        ht = xt.astype(jnp.bfloat16)
        lt = (xt - ht.astype(jnp.float32)).astype(jnp.bfloat16)
        right = slice(panel * PANEL, width)
        own[rows, at] = (
            jnp.dot(ht, high[:, right], preferred_element_type=jnp.float32)
            + jnp.dot(ht, low[:, right], preferred_element_type=jnp.float32)
            + jnp.dot(lt, high[:, right], preferred_element_type=jnp.float32)
        )

    for q in range(packed):
        rows = slice(q * PANEL, (q + 1) * PANEL)
        gram(q, rows, slice(q * PANEL, width))
        if q:
            gram(blocks - q, rows, slice(0, q * PANEL))

        @pl.when(jnp.logical_not(has_left))
        def _():
            for c in range(q * per_panel, (q + 1) * per_panel):
                to_right(own, c).start()

        @pl.when(jnp.logical_not(has_right))
        def _():
            for c in range(q * per_panel, (q + 1) * per_panel):
                to_left(own, c).start()

        if q == 1:
            near(0)
        if q == 2:
            near(1)
            far(0)
    for peer in peers:
        dest_copy(peer, front).start()
    for c in range(2, per_panel + 1):
        near(c)
        far(c - 1)

    def one_panel(panel, carry):
        base = pl.multiple_of(panel * PANEL, PANEL)
        folded = panel >= packed
        source = pl.ds(pl.multiple_of(jnp.where(folded, blocks - panel, panel) * PANEL, PANEL), PANEL)
        shift = jnp.where(folded, panel, 0)

        def total(j, carry):
            at = pl.ds(pl.multiple_of((j - shift) * PANEL, PANEL), PANEL)
            a_ref[pl.ds(base, PANEL), pl.ds(pl.multiple_of(j * PANEL, PANEL), PANEL)] = (
                own[source, at] + in_l[source, at] + in_r[source, at]
            )
            return carry

        lax.fori_loop(panel, blocks, total, 0)

        def earlier(q, carry):
            done = pl.ds(pl.multiple_of(q * PANEL, PANEL), PANEL)
            head = a_ref[done, pl.ds(base, PANEL)].T
            a_ref[pl.ds(base, PANEL), :] = a_ref[pl.ds(base, PANEL), :] - jnp.dot(
                head, a_ref[done, :], precision=lax.Precision.HIGH, preferred_element_type=jnp.float32
            )
            return carry

        lax.fori_loop(0, panel, earlier, 0)
        for group in range(PANEL // SUB):
            for part in range(SUB // CHUNK):
                c = (panel + 1) * per_panel + group * (SUB // CHUNK) + part

                @pl.when(c + 1 < chunks)
                def _():
                    near(c + 1)

                @pl.when(c < chunks)
                def _():
                    far(c)

            for t in range(SUB // STRIP):
                strip = group * (SUB // STRIP) + t
                start = pl.multiple_of(base + strip * STRIP, STRIP)
                rows, sub, lanes = factor_strip(a_ref, start, panel, strip, width)
                for later in range(strip + 1, (group + 1) * (SUB // STRIP)):
                    below = pl.multiple_of(base + later * STRIP, STRIP)
                    picked = lanes == sub + later * STRIP
                    mult = [
                        jnp.sum(jnp.where(picked, rows[k][blocks], 0.0), axis=1, keepdims=True)
                        for k in range(STRIP)
                    ]
                    for b in range(blocks):
                        at = (pl.ds(below, STRIP), slice(b * PANEL, (b + 1) * PANEL))
                        terms = [mult[k] * rows[k][b] for k in range(STRIP)]
                        while len(terms) > 1:
                            terms = [x + y for x, y in zip(terms[::2], terms[1::2])]
                        a_ref[at] = a_ref[at] - terms[0]
            if group < PANEL // SUB - 1:
                done = pl.ds(pl.multiple_of(base + group * SUB, SUB), SUB)
                left = PANEL - (group + 1) * SUB
                head = a_ref[done, pl.ds(base, PANEL)].T[(group + 1) * SUB:, :]
                rest = pl.ds(pl.multiple_of(base + (group + 1) * SUB, SUB), left)
                a_ref[rest, :] = a_ref[rest, :] - jnp.dot(
                    head, a_ref[done, :], precision=lax.Precision.HIGH, preferred_element_type=jnp.float32
                )

        @pl.when(panel == last_panel)
        def _():
            send_rows()

        return carry

    lax.fori_loop(0, blocks, one_panel, 0)
    pivot_count = pivot_ref.shape[0]
    row = lax.broadcasted_iota(jnp.int32, (pivot_count, width), 0) + me * pivot_count
    pivot_ref[...] = jnp.where(
        row <= lax.broadcasted_iota(jnp.int32, (pivot_count, width), 1),
        a_ref[pl.ds(pl.multiple_of(me * pivot_count, STRIP), pivot_count), :],
        0.0,
    )
    dest_in[slots_of(front), :] = dest_ref[slots_of(front), :]
    for peer in peers:
        dest_copy(peer, peer).wait_recv()
    target = lax.broadcasted_iota(jnp.int32, (slots, PANEL), 1).astype(jnp.float32) + 1.0
    place = (dest_in[...] == target).astype(jnp.float32).T[:PR_DEV, :]
    for peer in peers:
        def arrived(j, carry, peer=peer):
            row_copy(peer, peer, j).wait_recv()
            return carry

        lax.fori_loop(first_block, contrib_blocks, arrived, 0)
    sum_ref[...] = jnp.dot(place, rows_in[...], precision=highest, preferred_element_type=jnp.float32)

    for peer in peers:
        dest_copy(peer, peer).wait_send()

        def left(j, carry, peer=peer):
            row_copy(peer, peer, j).wait_send()
            return carry

        lax.fori_loop(first_block, contrib_blocks, left, 0)

    def finish(c, carry):
        @pl.when(has_right)
        def _():
            to_right(out_r, c).wait_send()

        @pl.when(has_left)
        def _():
            to_left(out_l, c).wait_send()

        return carry

    lax.fori_loop(0, chunks, finish, 0)


def front_factor(x, select, dest, fronts, pivot_count):
    rows, width = x.shape
    packed = (width // PANEL + 1) // 2 * PANEL
    slots = select.shape[0]
    contrib_width = width - PIV
    sums = pltpu.VMEM((packed, width), jnp.float32)
    sems = pltpu.SemaphoreType.DMA((packed // CHUNK,))
    row_sems = pltpu.SemaphoreType.DMA((fronts, contrib_width // PANEL))
    dest_sems = pltpu.SemaphoreType.DMA((fronts,))
    return pl.pallas_call(
        front_kernel,
        out_shape=(
            jax.ShapeDtypeStruct((pivot_count, width), jnp.float32),
            jax.ShapeDtypeStruct((PR_DEV, contrib_width), jnp.float32),
        ),
        in_specs=[pl.BlockSpec(memory_space=pltpu.VMEM)] * 3,
        out_specs=[pl.BlockSpec(memory_space=pltpu.VMEM)] * 2,
        scratch_shapes=[pltpu.VMEM((width, width), jnp.float32)]
        + [pltpu.VMEM((rows, width), jnp.bfloat16)] * 2
        + [sums] * 5
        + [pltpu.VMEM((slots, contrib_width), jnp.float32)] * 2
        + [pltpu.VMEM((slots, PANEL), jnp.float32)]
        + [sems] * 4
        + [row_sems] * 2
        + [dest_sems] * 2,
        compiler_params=pltpu.CompilerParams(
            vmem_limit_bytes=48 * 1024 * 1024, collective_id=0, has_side_effects=True
        ),
        name="front_factor",
    )(x, select, dest)


def shards(stacked, row_owner, dest_local):
    contrib_count = row_owner.shape[1]
    pivot_count = PIV // lax.axis_size("leaf")
    owners = row_owner[0, :, 0]
    targets = dest_local[0]
    fronts = lax.axis_size("front")
    capacity = max(2, (2 * contrib_count + fronts - 1) // fronts)
    capacity = (capacity + STRIP - 1) // STRIP * STRIP
    same_owner = owners[:, None] == owners[None, :]
    earlier = lax.broadcasted_iota(
        jnp.int32, (contrib_count, contrib_count), 1
    ) < lax.broadcasted_iota(jnp.int32, (contrib_count, contrib_count), 0)
    slot_rank = jnp.sum((same_owner & earlier).astype(jnp.int32), axis=1)
    slot_index = owners * capacity + slot_rank
    chosen = slot_index[None, :] == lax.broadcasted_iota(jnp.int32, (fronts * capacity, contrib_count), 0)
    send_dest = jnp.sum(jnp.where(chosen, (targets + 1)[None, :], 0), axis=1).astype(jnp.float32)
    pivot_part, assembled = front_factor(
        stacked[0],
        chosen.astype(jnp.float32),
        jnp.broadcast_to(send_dest[:, None], (fronts * capacity, PANEL)),
        fronts,
        pivot_count,
    )
    return (pivot_part[None], assembled[None])


def solution(mesh):
    return jax.shard_map(
        shards,
        mesh=mesh,
        in_specs=(P("front", "leaf", None), P("front", "leaf", None), P("front", "leaf")),
        out_specs=(P("front", "leaf", None), P("front", "leaf", None)),
        check_vma=False,
    )
```

```python
import functools
import jax
import jax.numpy as jnp
from jax import lax
from jax.experimental import pallas as pl
from jax.experimental.pallas import tpu as pltpu
from jax.sharding import PartitionSpec as P

PIV = 256
PR_DEV = 64
STRIP = 8
SUB = 32
PANEL = 128
CHUNK = 32
MESH = pl.DeviceIdType.MESH


highest = lax.Precision.HIGHEST


def factor_strip(a_ref, start, panel, strip, width):
    blocks = width // PANEL
    diag = a_ref[pl.ds(start, STRIP), pl.ds(pl.multiple_of(panel * PANEL, PANEL), PANEL)]
    c = {}
    for k in range(STRIP):
        lane = strip * STRIP + k
        column = jnp.broadcast_to(diag[:, lane:lane + 1], (STRIP, PANEL))
        for i in range(k, STRIP):
            c[i, k] = jnp.broadcast_to(column[i:i + 1, :], (STRIP, PANEL))
    body = [a_ref[pl.ds(start, STRIP), b * PANEL:(b + 1) * PANEL] for b in range(blocks)]
    body.append(diag)
    rows = [[jnp.broadcast_to(x[k:k + 1, :], (STRIP, PANEL)) for x in body] for k in range(STRIP)]
    for k in range(STRIP):
        inv = lax.rsqrt(c[k, k])
        rows[k] = [x * inv for x in rows[k]]
        for i in range(k + 1, STRIP):
            c[i, k] = c[i, k] * inv
        for i in range(k + 1, STRIP):
            for j in range(k + 1, i + 1):
                c[i, j] = c[i, j] - c[i, k] * c[j, k]
            rows[i] = [x - c[i, k] * y for x, y in zip(rows[i], rows[k])]
    sub = lax.broadcasted_iota(jnp.int32, (STRIP, PANEL), 0)
    lanes = lax.broadcasted_iota(jnp.int32, (STRIP, PANEL), 1)
    for b in range(blocks):
        out = rows[0][b]
        for k in range(1, STRIP):
            out = jnp.where(sub == k, rows[k][b], out)
        a_ref[pl.ds(start, STRIP), b * PANEL:(b + 1) * PANEL] = out
    return rows, sub, lanes


def front_kernel(
    x_ref, select_ref, dest_ref, pivot_ref, sum_ref, a_ref, update, high, low, own, in_l, in_r, out_l, out_r,
    rows_out, rows_in, dest_in, send_l, recv_l, send_r, recv_r, row_send, row_recv, dest_send, dest_recv,
):
    width = a_ref.shape[0]
    blocks = width // PANEL
    packed = (blocks + 1) // 2
    chunks = packed * PANEL // CHUNK
    per_panel = PANEL // CHUNK
    me, n = lax.axis_index("leaf"), lax.axis_size("leaf")
    has_left, has_right = me > 0, me < n - 1
    front, fronts = lax.axis_index("front"), lax.axis_size("front")
    slots, contrib_count = select_ref.shape
    capacity = slots // fronts
    contrib_blocks = (width - PIV) // PANEL
    first_block = me * contrib_count // PANEL
    last_panel = (PIV + (me + 1) * contrib_count - 1) // PANEL
    peers = [lax.rem(front + d, fronts) for d in range(1, fronts)]

    barrier = pltpu.get_barrier_semaphore()

    @pl.when(has_left)
    def _():
        pl.semaphore_signal(barrier, inc=1, device_id={"leaf": me - 1}, device_id_type=MESH)

    @pl.when(has_right)
    def _():
        pl.semaphore_signal(barrier, inc=1, device_id={"leaf": me + 1}, device_id_type=MESH)

    rows_in[...] = jnp.zeros_like(rows_in)
    for peer in peers:
        pl.semaphore_signal(barrier, inc=1, device_id={"front": peer}, device_id_type=MESH)

    @pl.when(jnp.logical_not(has_left))
    def _():
        in_l[...] = jnp.zeros_like(in_l)

    @pl.when(jnp.logical_not(has_right))
    def _():
        in_r[...] = jnp.zeros_like(in_r)

    a_ref[...] = jnp.zeros_like(a_ref)
    update[...] = jnp.zeros_like(update)
    high[...] = x_ref[...].astype(jnp.bfloat16)
    low[...] = (x_ref[...] - high[...].astype(jnp.float32)).astype(jnp.bfloat16)

    inner = jnp.logical_and(has_left, has_right)

    @pl.when(inner)
    def _():
        pl.semaphore_wait(barrier, 2 + fronts - 1)

    @pl.when(jnp.logical_not(inner))
    def _():
        pl.semaphore_wait(barrier, 1 + fronts - 1)

    def slots_of(g):
        return pl.ds(pl.multiple_of(g * capacity, STRIP), capacity)

    def dest_copy(to, src):
        return pltpu.make_async_remote_copy(
            src_ref=dest_ref.at[slots_of(to)], dst_ref=dest_in.at[slots_of(src)],
            send_sem=dest_send.at[to], recv_sem=dest_recv.at[src],
            device_id={"front": to}, device_id_type=MESH,
        )

    def row_copy(to, src, j):
        at = pl.ds(pl.multiple_of(j * PANEL, PANEL), PANEL)
        return pltpu.make_async_remote_copy(
            src_ref=rows_out.at[slots_of(to), at], dst_ref=rows_in.at[slots_of(src), at],
            send_sem=row_send.at[to, j], recv_sem=row_recv.at[src, j],
            device_id={"front": to}, device_id_type=MESH,
        )

    def send_rows():
        start = pl.multiple_of(PIV + me * contrib_count, STRIP)
        shape = (contrib_count, width - PIV)
        row = lax.broadcasted_iota(jnp.int32, shape, 0) + me * contrib_count
        rows = jnp.where(
            row <= lax.broadcasted_iota(jnp.int32, shape, 1), a_ref[pl.ds(start, contrib_count), PIV:], 0.0
        )
        rows_out[...] = jnp.dot(
            select_ref[...], rows, precision=highest, preferred_element_type=jnp.float32
        )
        for peer in peers:
            def one(j, carry, peer=peer):
                row_copy(peer, front, j).start()
                return carry

            lax.fori_loop(first_block, contrib_blocks, one, 0)
        rows_in[slots_of(front), :] = rows_out[slots_of(front), :]

    def rows_of(c):
        return pl.ds(pl.multiple_of(c * CHUNK, CHUNK), CHUNK)

    def to_right(src, c):
        return pltpu.make_async_remote_copy(
            src_ref=src.at[rows_of(c)], dst_ref=in_l.at[rows_of(c)],
            send_sem=send_r.at[c], recv_sem=recv_l.at[c],
            device_id={"leaf": me + 1}, device_id_type=MESH,
        )

    def to_left(src, c):
        return pltpu.make_async_remote_copy(
            src_ref=src.at[rows_of(c)], dst_ref=in_r.at[rows_of(c)],
            send_sem=send_l.at[c], recv_sem=recv_r.at[c],
            device_id={"leaf": me - 1}, device_id_type=MESH,
        )

    def from_left(c):
        @pl.when(has_left)
        def _():
            to_right(out_r, c).wait_recv()

            @pl.when(has_right)
            def _():
                out_r[rows_of(c), :] = own[rows_of(c), :] + in_l[rows_of(c), :]
                to_right(out_r, c).start()

    def from_right(c):
        @pl.when(has_right)
        def _():
            to_left(out_l, c).wait_recv()

            @pl.when(has_left)
            def _():
                out_l[rows_of(c), :] = own[rows_of(c), :] + in_r[rows_of(c), :]
                to_left(out_l, c).start()

    first_half = 2 * me < n

    def near(c):
        @pl.when(first_half)
        def _():
            from_left(c)

        @pl.when(jnp.logical_not(first_half))
        def _():
            from_right(c)

    def far(c):
        @pl.when(first_half)
        def _():
            from_right(c)

        @pl.when(jnp.logical_not(first_half))
        def _():
            from_left(c)

    def gram(panel, rows, at):
        cols = slice(panel * PANEL, (panel + 1) * PANEL)
        xt = x_ref[:, cols].T
        ht = xt.astype(jnp.bfloat16)
        lt = (xt - ht.astype(jnp.float32)).astype(jnp.bfloat16)
        right = slice(panel * PANEL, width)
        own[rows, at] = (
            jnp.dot(ht, high[:, right], preferred_element_type=jnp.float32)
            + jnp.dot(ht, low[:, right], preferred_element_type=jnp.float32)
            + jnp.dot(lt, high[:, right], preferred_element_type=jnp.float32)
        )

    def slot(k):
        if k <= per_panel:
            near(k)
            if k:
                far(k - 1)

    for q in range(packed):
        rows = slice(q * PANEL, (q + 1) * PANEL)
        gram(q, rows, slice(q * PANEL, width))
        if q:
            slot(2 * q - 2)
            gram(blocks - q, rows, slice(0, q * PANEL))

        @pl.when(jnp.logical_not(has_left))
        def _():
            for c in range(q * per_panel, (q + 1) * per_panel):
                to_right(own, c).start()

        @pl.when(jnp.logical_not(has_right))
        def _():
            for c in range(q * per_panel, (q + 1) * per_panel):
                to_left(own, c).start()

        if q:
            slot(2 * q - 1)
    for peer in peers:
        dest_copy(peer, front).start()
    for k in range(2 * packed - 2, per_panel + 1):
        slot(k)

    def one_panel(panel, carry):
        base = pl.multiple_of(panel * PANEL, PANEL)
        folded = panel >= packed
        source = pl.ds(pl.multiple_of(jnp.where(folded, blocks - panel, panel) * PANEL, PANEL), PANEL)
        shift = jnp.where(folded, panel, 0)

        def total(j, carry):
            at = pl.ds(pl.multiple_of((j - shift) * PANEL, PANEL), PANEL)
            a_ref[pl.ds(base, PANEL), pl.ds(pl.multiple_of(j * PANEL, PANEL), PANEL)] = (
                own[source, at] + in_l[source, at] + in_r[source, at]
            ) - update[:, pl.ds(pl.multiple_of(j * PANEL, PANEL), PANEL)]
            return carry

        lax.fori_loop(panel, blocks, total, 0)

        @pl.when(panel > 0)
        def _():
            done = pl.ds(pl.multiple_of(base - PANEL, PANEL), PANEL)
            head = a_ref[done, pl.ds(base, PANEL)].T
            a_ref[pl.ds(base, PANEL), :] = a_ref[pl.ds(base, PANEL), :] - jnp.dot(
                head, a_ref[done, :], precision=lax.Precision.HIGH, preferred_element_type=jnp.float32
            )

        following = pl.multiple_of(jnp.minimum(panel + 1, blocks - 1) * PANEL, PANEL)
        batch = -(-(blocks - 1) // (PANEL // SUB)) * PANEL
        for group in range(PANEL // SUB):
            for part in range(SUB // CHUNK):
                c = (panel + 1) * per_panel + group * (SUB // CHUNK) + part

                @pl.when(c + 1 < chunks)
                def _():
                    near(c + 1)

                @pl.when(c < chunks)
                def _():
                    far(c)

            if group * batch < (blocks - 1) * PANEL:
                done = slice(group * batch, min((group + 1) * batch, (blocks - 1) * PANEL))
                head = a_ref[done, pl.ds(following, PANEL)]
                row = lax.broadcasted_iota(jnp.int32, head.shape, 0) + group * batch
                part = jnp.dot(
                    jnp.where(row < base, head, 0.0).T, a_ref[done, :],
                    precision=lax.Precision.HIGH, preferred_element_type=jnp.float32,
                )
                update[...] = update[...] + part if group else part
            for t in range(SUB // STRIP):
                strip = group * (SUB // STRIP) + t
                start = pl.multiple_of(base + strip * STRIP, STRIP)
                rows, sub, lanes = factor_strip(a_ref, start, panel, strip, width)
                for later in range(strip + 1, (group + 1) * (SUB // STRIP)):
                    below = pl.multiple_of(base + later * STRIP, STRIP)
                    picked = lanes == sub + later * STRIP
                    mult = [
                        jnp.sum(jnp.where(picked, rows[k][blocks], 0.0), axis=1, keepdims=True)
                        for k in range(STRIP)
                    ]
                    for b in range(blocks):
                        at = (pl.ds(below, STRIP), slice(b * PANEL, (b + 1) * PANEL))
                        terms = [mult[k] * rows[k][b] for k in range(STRIP)]
                        while len(terms) > 1:
                            terms = [x + y for x, y in zip(terms[::2], terms[1::2])]
                        a_ref[at] = a_ref[at] - terms[0]
            if group < PANEL // SUB - 1:
                done = pl.ds(pl.multiple_of(base + group * SUB, SUB), SUB)
                left = PANEL - (group + 1) * SUB
                head = a_ref[done, pl.ds(base, PANEL)].T[(group + 1) * SUB:, :]
                rest = pl.ds(pl.multiple_of(base + (group + 1) * SUB, SUB), left)
                a_ref[rest, :] = a_ref[rest, :] - jnp.dot(
                    head, a_ref[done, :], precision=lax.Precision.HIGH, preferred_element_type=jnp.float32
                )

        @pl.when(panel == last_panel)
        def _():
            send_rows()

        return carry

    lax.fori_loop(0, blocks, one_panel, 0)
    pivot_count = pivot_ref.shape[0]
    row = lax.broadcasted_iota(jnp.int32, (pivot_count, width), 0) + me * pivot_count
    pivot_ref[...] = jnp.where(
        row <= lax.broadcasted_iota(jnp.int32, (pivot_count, width), 1),
        a_ref[pl.ds(pl.multiple_of(me * pivot_count, STRIP), pivot_count), :],
        0.0,
    )
    dest_in[slots_of(front), :] = dest_ref[slots_of(front), :]
    for peer in peers:
        dest_copy(peer, peer).wait_recv()
    target = lax.broadcasted_iota(jnp.int32, (slots, PANEL), 1).astype(jnp.float32) + 1.0
    place = (dest_in[...] == target).astype(jnp.float32).T[:PR_DEV, :]
    for peer in peers:
        def arrived(j, carry, peer=peer):
            row_copy(peer, peer, j).wait_recv()
            return carry

        lax.fori_loop(first_block, contrib_blocks, arrived, 0)
    sum_ref[...] = jnp.dot(place, rows_in[...], precision=highest, preferred_element_type=jnp.float32)

    for peer in peers:
        dest_copy(peer, peer).wait_send()

        def left(j, carry, peer=peer):
            row_copy(peer, peer, j).wait_send()
            return carry

        lax.fori_loop(first_block, contrib_blocks, left, 0)

    def finish(c, carry):
        @pl.when(has_right)
        def _():
            to_right(out_r, c).wait_send()

        @pl.when(has_left)
        def _():
            to_left(out_l, c).wait_send()

        return carry

    lax.fori_loop(0, chunks, finish, 0)


def front_factor(x, select, dest, fronts, pivot_count):
    rows, width = x.shape
    packed = (width // PANEL + 1) // 2 * PANEL
    slots = select.shape[0]
    contrib_width = width - PIV
    sums = pltpu.VMEM((packed, width), jnp.float32)
    sems = pltpu.SemaphoreType.DMA((packed // CHUNK,))
    row_sems = pltpu.SemaphoreType.DMA((fronts, contrib_width // PANEL))
    dest_sems = pltpu.SemaphoreType.DMA((fronts,))
    return pl.pallas_call(
        front_kernel,
        out_shape=(
            jax.ShapeDtypeStruct((pivot_count, width), jnp.float32),
            jax.ShapeDtypeStruct((PR_DEV, contrib_width), jnp.float32),
        ),
        in_specs=[pl.BlockSpec(memory_space=pltpu.VMEM)] * 3,
        out_specs=[pl.BlockSpec(memory_space=pltpu.VMEM)] * 2,
        scratch_shapes=[pltpu.VMEM((width, width), jnp.float32), pltpu.VMEM((PANEL, width), jnp.float32)]
        + [pltpu.VMEM((rows, width), jnp.bfloat16)] * 2
        + [sums] * 5
        + [pltpu.VMEM((slots, contrib_width), jnp.float32)] * 2
        + [pltpu.VMEM((slots, PANEL), jnp.float32)]
        + [sems] * 4
        + [row_sems] * 2
        + [dest_sems] * 2,
        compiler_params=pltpu.CompilerParams(
            vmem_limit_bytes=48 * 1024 * 1024, collective_id=0, has_side_effects=True
        ),
        name="front_factor",
    )(x, select, dest)


def shards(stacked, row_owner, dest_local):
    contrib_count = row_owner.shape[1]
    pivot_count = PIV // lax.axis_size("leaf")
    owners = row_owner[0, :, 0]
    targets = dest_local[0]
    fronts = lax.axis_size("front")
    capacity = max(2, (2 * contrib_count + fronts - 1) // fronts)
    capacity = (capacity + STRIP - 1) // STRIP * STRIP
    same_owner = owners[:, None] == owners[None, :]
    earlier = lax.broadcasted_iota(
        jnp.int32, (contrib_count, contrib_count), 1
    ) < lax.broadcasted_iota(jnp.int32, (contrib_count, contrib_count), 0)
    slot_rank = jnp.sum((same_owner & earlier).astype(jnp.int32), axis=1)
    slot_index = owners * capacity + slot_rank
    chosen = slot_index[None, :] == lax.broadcasted_iota(jnp.int32, (fronts * capacity, contrib_count), 0)
    send_dest = jnp.sum(jnp.where(chosen, (targets + 1)[None, :], 0), axis=1).astype(jnp.float32)
    pivot_part, assembled = front_factor(
        stacked[0],
        chosen.astype(jnp.float32),
        jnp.broadcast_to(send_dest[:, None], (fronts * capacity, PANEL)),
        fronts,
        pivot_count,
    )
    return (pivot_part[None], assembled[None])


def solution(mesh):
    return jax.shard_map(
        shards,
        mesh=mesh,
        in_specs=(P("front", "leaf", None), P("front", "leaf", None), P("front", "leaf")),
        out_specs=(P("front", "leaf", None), P("front", "leaf", None)),
        check_vma=False,
    )
```

```python
import functools
import jax
import jax.numpy as jnp
from jax import lax
from jax.experimental import pallas as pl
from jax.experimental.pallas import tpu as pltpu
from jax.sharding import PartitionSpec as P

PIV = 256
PR_DEV = 64
STRIP = 8
SUB = 32
PANEL = 128
CHUNK = 32
MESH = pl.DeviceIdType.MESH


highest = lax.Precision.HIGHEST


def factor_strip(a_ref, start, panel, strip, width):
    blocks = width // PANEL
    diag = a_ref[pl.ds(start, STRIP), pl.ds(pl.multiple_of(panel * PANEL, PANEL), PANEL)]
    c = {}
    for k in range(STRIP):
        lane = strip * STRIP + k
        column = jnp.broadcast_to(diag[:, lane:lane + 1], (STRIP, PANEL))
        for i in range(k, STRIP):
            c[i, k] = jnp.broadcast_to(column[i:i + 1, :], (STRIP, PANEL))
    body = [a_ref[pl.ds(start, STRIP), b * PANEL:(b + 1) * PANEL] for b in range(blocks)]
    body.append(diag)
    rows = [[jnp.broadcast_to(x[k:k + 1, :], (STRIP, PANEL)) for x in body] for k in range(STRIP)]
    for k in range(STRIP):
        inv = lax.rsqrt(c[k, k])
        rows[k] = [x * inv for x in rows[k]]
        for i in range(k + 1, STRIP):
            c[i, k] = c[i, k] * inv
        for i in range(k + 1, STRIP):
            for j in range(k + 1, i + 1):
                c[i, j] = c[i, j] - c[i, k] * c[j, k]
            rows[i] = [x - c[i, k] * y for x, y in zip(rows[i], rows[k])]
    sub = lax.broadcasted_iota(jnp.int32, (STRIP, PANEL), 0)
    lanes = lax.broadcasted_iota(jnp.int32, (STRIP, PANEL), 1)
    for b in range(blocks):
        out = rows[0][b]
        for k in range(1, STRIP):
            out = jnp.where(sub == k, rows[k][b], out)
        a_ref[pl.ds(start, STRIP), b * PANEL:(b + 1) * PANEL] = out
    return rows, sub, lanes


def one_hot_dot(picks, values):
    total = None
    for _ in range(3):
        piece = values.astype(jnp.bfloat16)
        values = values - piece.astype(jnp.float32)
        part = jnp.dot(picks, piece, preferred_element_type=jnp.float32)
        total = part if total is None else total + part
    return total


def front_kernel(
    x_ref, owner_ref, target_ref, pivot_ref, sum_ref, a_ref, update, select, dest_ref, high, low, own, in_l, in_r, out_l, out_r,
    rows_out, rows_in, dest_in, send_l, recv_l, send_r, recv_r, row_send, row_recv, dest_send, dest_recv,
):
    width = a_ref.shape[0]
    blocks = width // PANEL
    packed = (blocks + 1) // 2
    chunks = packed * PANEL // CHUNK
    per_panel = PANEL // CHUNK
    me, n = lax.axis_index("leaf"), lax.axis_size("leaf")
    has_left, has_right = me > 0, me < n - 1
    front, fronts = lax.axis_index("front"), lax.axis_size("front")
    slots, contrib_count = select.shape
    capacity = slots // fronts
    contrib_blocks = (width - PIV) // PANEL
    first_block = me * contrib_count // PANEL
    last_panel = (PIV + (me + 1) * contrib_count - 1) // PANEL
    peers = [lax.rem(front + d, fronts) for d in range(1, fronts)]

    barrier = pltpu.get_barrier_semaphore()

    @pl.when(has_left)
    def _():
        pl.semaphore_signal(barrier, inc=1, device_id={"leaf": me - 1}, device_id_type=MESH)

    @pl.when(has_right)
    def _():
        pl.semaphore_signal(barrier, inc=1, device_id={"leaf": me + 1}, device_id_type=MESH)

    rows_in[...] = jnp.zeros_like(rows_in)
    for peer in peers:
        pl.semaphore_signal(barrier, inc=1, device_id={"front": peer}, device_id_type=MESH)

    @pl.when(jnp.logical_not(has_left))
    def _():
        in_l[...] = jnp.zeros_like(in_l)

    @pl.when(jnp.logical_not(has_right))
    def _():
        in_r[...] = jnp.zeros_like(in_r)

    a_ref[...] = jnp.zeros_like(a_ref)
    update[...] = jnp.zeros_like(update)
    sum_ref[...] = jnp.zeros_like(sum_ref)
    high[...] = x_ref[...].astype(jnp.bfloat16)
    low[...] = (x_ref[...] - high[...].astype(jnp.float32)).astype(jnp.bfloat16)

    inner = jnp.logical_and(has_left, has_right)

    @pl.when(inner)
    def _():
        pl.semaphore_wait(barrier, 2 + fronts - 1)

    @pl.when(jnp.logical_not(inner))
    def _():
        pl.semaphore_wait(barrier, 1 + fronts - 1)

    def slots_of(g):
        return pl.ds(pl.multiple_of(g * capacity, STRIP), capacity)

    def dest_copy(to, src):
        return pltpu.make_async_remote_copy(
            src_ref=dest_ref.at[slots_of(to)], dst_ref=dest_in.at[slots_of(src)],
            send_sem=dest_send.at[to], recv_sem=dest_recv.at[src],
            device_id={"front": to}, device_id_type=MESH,
        )

    def row_copy(to, src, j):
        at = pl.ds(pl.multiple_of(j * PANEL, PANEL), PANEL)
        return pltpu.make_async_remote_copy(
            src_ref=rows_out.at[slots_of(to), at], dst_ref=rows_in.at[slots_of(src), at],
            send_sem=row_send.at[to, j], recv_sem=row_recv.at[src, j],
            device_id={"front": to}, device_id_type=MESH,
        )

    def send_rows():
        start = pl.multiple_of(PIV + me * contrib_count, STRIP)
        row = lax.broadcasted_iota(jnp.int32, (contrib_count, PANEL), 0) + me * contrib_count
        lane = lax.broadcasted_iota(jnp.int32, (contrib_count, PANEL), 1)

        def block(j, carry):
            at = pl.ds(pl.multiple_of(j * PANEL, PANEL), PANEL)
            rows = a_ref[pl.ds(start, contrib_count), pl.ds(pl.multiple_of(PIV + j * PANEL, PANEL), PANEL)]
            rows_out[:, at] = one_hot_dot(select[...], jnp.where(row <= lane + j * PANEL, rows, 0.0))
            for peer in peers:
                row_copy(peer, front, j).start()
            rows_in[slots_of(front), at] = rows_out[slots_of(front), at]
            return carry

        lax.fori_loop(first_block, contrib_blocks, block, 0)

    def prepare_slots():
        mine = jnp.broadcast_to(owner_ref[...].astype(jnp.float32), (contrib_count, PANEL))
        owner_row = mine.T[0:1, :]
        square = (contrib_count, contrib_count)
        before = lax.broadcasted_iota(jnp.int32, square, 0) < lax.broadcasted_iota(jnp.int32, square, 1)
        same = owner_ref[...].astype(jnp.float32) == owner_row
        rank = jnp.sum(jnp.where(same & before, 1.0, 0.0), axis=0, keepdims=True)
        slot_row = owner_row * capacity + rank
        chosen = lax.broadcasted_iota(jnp.int32, (slots, contrib_count), 0).astype(jnp.float32) == slot_row
        select[...] = jnp.where(chosen, 1.0, 0.0).astype(jnp.bfloat16)
        wanted = jnp.where(chosen, target_ref[...].astype(jnp.float32) + 1.0, 0.0)
        dest_ref[...] = jnp.broadcast_to(jnp.sum(wanted, axis=1, keepdims=True), dest_ref.shape)
        for peer in peers:
            dest_copy(peer, front).start()

    def rows_of(c):
        return pl.ds(pl.multiple_of(c * CHUNK, CHUNK), CHUNK)

    def to_right(src, c):
        return pltpu.make_async_remote_copy(
            src_ref=src.at[rows_of(c)], dst_ref=in_l.at[rows_of(c)],
            send_sem=send_r.at[c], recv_sem=recv_l.at[c],
            device_id={"leaf": me + 1}, device_id_type=MESH,
        )

    def to_left(src, c):
        return pltpu.make_async_remote_copy(
            src_ref=src.at[rows_of(c)], dst_ref=in_r.at[rows_of(c)],
            send_sem=send_l.at[c], recv_sem=recv_r.at[c],
            device_id={"leaf": me - 1}, device_id_type=MESH,
        )

    def from_left(c):
        @pl.when(has_left)
        def _():
            to_right(out_r, c).wait_recv()

            @pl.when(has_right)
            def _():
                out_r[rows_of(c), :] = own[rows_of(c), :] + in_l[rows_of(c), :]
                to_right(out_r, c).start()

    def from_right(c):
        @pl.when(has_right)
        def _():
            to_left(out_l, c).wait_recv()

            @pl.when(has_left)
            def _():
                out_l[rows_of(c), :] = own[rows_of(c), :] + in_r[rows_of(c), :]
                to_left(out_l, c).start()

    first_half = 2 * me < n

    def near(c):
        @pl.when(first_half)
        def _():
            from_left(c)

        @pl.when(jnp.logical_not(first_half))
        def _():
            from_right(c)

    def far(c):
        @pl.when(first_half)
        def _():
            from_right(c)

        @pl.when(jnp.logical_not(first_half))
        def _():
            from_left(c)

    def gram(panel, rows, at):
        cols = slice(panel * PANEL, (panel + 1) * PANEL)
        xt = x_ref[:, cols].T
        ht = xt.astype(jnp.bfloat16)
        lt = (xt - ht.astype(jnp.float32)).astype(jnp.bfloat16)
        right = slice(panel * PANEL, width)
        own[rows, at] = (
            jnp.dot(ht, high[:, right], preferred_element_type=jnp.float32)
            + jnp.dot(ht, low[:, right], preferred_element_type=jnp.float32)
            + jnp.dot(lt, high[:, right], preferred_element_type=jnp.float32)
        )

    def slot(k):
        if k <= per_panel:
            near(k)
            if k:
                far(k - 1)

    for q in range(packed):
        rows = slice(q * PANEL, (q + 1) * PANEL)
        gram(q, rows, slice(q * PANEL, width))
        if q:
            slot(2 * q - 2)
            gram(blocks - q, rows, slice(0, q * PANEL))

        @pl.when(jnp.logical_not(has_left))
        def _():
            for c in range(q * per_panel, (q + 1) * per_panel):
                to_right(own, c).start()

        @pl.when(jnp.logical_not(has_right))
        def _():
            for c in range(q * per_panel, (q + 1) * per_panel):
                to_left(own, c).start()

        if q:
            slot(2 * q - 1)
        else:
            prepare_slots()
    for k in range(2 * packed - 2, per_panel + 1):
        slot(k)

    def one_panel(panel, carry):
        base = pl.multiple_of(panel * PANEL, PANEL)
        folded = panel >= packed
        source = pl.ds(pl.multiple_of(jnp.where(folded, blocks - panel, panel) * PANEL, PANEL), PANEL)
        shift = jnp.where(folded, panel, 0)

        def total(j, carry):
            at = pl.ds(pl.multiple_of((j - shift) * PANEL, PANEL), PANEL)
            a_ref[pl.ds(base, PANEL), pl.ds(pl.multiple_of(j * PANEL, PANEL), PANEL)] = (
                own[source, at] + in_l[source, at] + in_r[source, at]
            ) - update[:, pl.ds(pl.multiple_of(j * PANEL, PANEL), PANEL)]
            return carry

        lax.fori_loop(panel, blocks, total, 0)

        @pl.when(panel > 0)
        def _():
            done = pl.ds(pl.multiple_of(base - PANEL, PANEL), PANEL)
            head = a_ref[done, pl.ds(base, PANEL)].T
            a_ref[pl.ds(base, PANEL), :] = a_ref[pl.ds(base, PANEL), :] - jnp.dot(
                head, a_ref[done, :], precision=lax.Precision.HIGH, preferred_element_type=jnp.float32
            )

        following = pl.multiple_of(jnp.minimum(panel + 1, blocks - 1) * PANEL, PANEL)
        batch = -(-(blocks - 1) // (PANEL // SUB)) * PANEL
        for group in range(PANEL // SUB):
            for part in range(SUB // CHUNK):
                c = (panel + 1) * per_panel + group * (SUB // CHUNK) + part

                @pl.when(c + 1 < chunks)
                def _():
                    near(c + 1)

                @pl.when(c < chunks)
                def _():
                    far(c)

            if group * batch < (blocks - 1) * PANEL:
                done = slice(group * batch, min((group + 1) * batch, (blocks - 1) * PANEL))
                head = a_ref[done, pl.ds(following, PANEL)]
                row = lax.broadcasted_iota(jnp.int32, head.shape, 0) + group * batch
                part = jnp.dot(
                    jnp.where(row < base, head, 0.0).T, a_ref[done, :],
                    precision=lax.Precision.HIGH, preferred_element_type=jnp.float32,
                )
                update[...] = update[...] + part if group else part
            for t in range(SUB // STRIP):
                strip = group * (SUB // STRIP) + t
                start = pl.multiple_of(base + strip * STRIP, STRIP)
                rows, sub, lanes = factor_strip(a_ref, start, panel, strip, width)
                for later in range(strip + 1, (group + 1) * (SUB // STRIP)):
                    below = pl.multiple_of(base + later * STRIP, STRIP)
                    picked = lanes == sub + later * STRIP
                    mult = [
                        jnp.sum(jnp.where(picked, rows[k][blocks], 0.0), axis=1, keepdims=True)
                        for k in range(STRIP)
                    ]
                    for b in range(blocks):
                        at = (pl.ds(below, STRIP), slice(b * PANEL, (b + 1) * PANEL))
                        terms = [mult[k] * rows[k][b] for k in range(STRIP)]
                        while len(terms) > 1:
                            terms = [x + y for x, y in zip(terms[::2], terms[1::2])]
                        a_ref[at] = a_ref[at] - terms[0]
            if group < PANEL // SUB - 1:
                done = pl.ds(pl.multiple_of(base + group * SUB, SUB), SUB)
                left = PANEL - (group + 1) * SUB
                head = a_ref[done, pl.ds(base, PANEL)].T[(group + 1) * SUB:, :]
                rest = pl.ds(pl.multiple_of(base + (group + 1) * SUB, SUB), left)
                a_ref[rest, :] = a_ref[rest, :] - jnp.dot(
                    head, a_ref[done, :], precision=lax.Precision.HIGH, preferred_element_type=jnp.float32
                )

        @pl.when(panel == last_panel)
        def _():
            send_rows()

        return carry

    lax.fori_loop(0, blocks, one_panel, 0)
    pivot_count = pivot_ref.shape[0]
    row = lax.broadcasted_iota(jnp.int32, (pivot_count, width), 0) + me * pivot_count
    pivot_ref[...] = jnp.where(
        row <= lax.broadcasted_iota(jnp.int32, (pivot_count, width), 1),
        a_ref[pl.ds(pl.multiple_of(me * pivot_count, STRIP), pivot_count), :],
        0.0,
    )
    dest_in[slots_of(front), :] = dest_ref[slots_of(front), :]
    for peer in peers:
        dest_copy(peer, peer).wait_recv()
    target = lax.broadcasted_iota(jnp.int32, (slots, PANEL), 1).astype(jnp.float32) + 1.0
    place = (dest_in[...] == target).astype(jnp.float32).T[:PR_DEV, :].astype(jnp.bfloat16)

    def arrived(j, carry):
        at = pl.ds(pl.multiple_of(j * PANEL, PANEL), PANEL)
        for peer in peers:
            row_copy(peer, peer, j).wait_recv()
        sum_ref[:, at] = one_hot_dot(place, rows_in[:, at])
        return carry

    lax.fori_loop(first_block, contrib_blocks, arrived, 0)

    for peer in peers:
        dest_copy(peer, peer).wait_send()

        def left(j, carry, peer=peer):
            row_copy(peer, peer, j).wait_send()
            return carry

        lax.fori_loop(first_block, contrib_blocks, left, 0)

    def finish(c, carry):
        @pl.when(has_right)
        def _():
            to_right(out_r, c).wait_send()

        @pl.when(has_left)
        def _():
            to_left(out_l, c).wait_send()

        return carry

    lax.fori_loop(0, chunks, finish, 0)


def front_factor(x, owners, targets, fronts, pivot_count, capacity):
    rows, width = x.shape
    packed = (width // PANEL + 1) // 2 * PANEL
    slots = fronts * capacity
    contrib_width = width - PIV
    sums = pltpu.VMEM((packed, width), jnp.float32)
    sems = pltpu.SemaphoreType.DMA((packed // CHUNK,))
    row_sems = pltpu.SemaphoreType.DMA((fronts, contrib_width // PANEL))
    dest_sems = pltpu.SemaphoreType.DMA((fronts,))
    return pl.pallas_call(
        front_kernel,
        out_shape=(
            jax.ShapeDtypeStruct((pivot_count, width), jnp.float32),
            jax.ShapeDtypeStruct((PR_DEV, contrib_width), jnp.float32),
        ),
        in_specs=[pl.BlockSpec(memory_space=pltpu.VMEM)] * 3,
        out_specs=[pl.BlockSpec(memory_space=pltpu.VMEM)] * 2,
        scratch_shapes=[pltpu.VMEM((width, width), jnp.float32), pltpu.VMEM((PANEL, width), jnp.float32)]
        + [pltpu.VMEM((slots, owners.shape[0]), jnp.bfloat16), pltpu.VMEM((slots, PANEL), jnp.float32)]
        + [pltpu.VMEM((rows, width), jnp.bfloat16)] * 2
        + [sums] * 5
        + [pltpu.VMEM((slots, contrib_width), jnp.float32)] * 2
        + [pltpu.VMEM((slots, PANEL), jnp.float32)]
        + [sems] * 4
        + [row_sems] * 2
        + [dest_sems] * 2,
        compiler_params=pltpu.CompilerParams(
            vmem_limit_bytes=48 * 1024 * 1024, collective_id=0, has_side_effects=True
        ),
        name="front_factor",
    )(x, owners, targets)


def shards(stacked, row_owner, dest_local):
    contrib_count = row_owner.shape[1]
    pivot_count = PIV // lax.axis_size("leaf")
    fronts = lax.axis_size("front")
    capacity = max(2, (2 * contrib_count + fronts - 1) // fronts)
    capacity = (capacity + STRIP - 1) // STRIP * STRIP
    pivot_part, assembled = front_factor(
        stacked[0], row_owner[0], dest_local, fronts, pivot_count, capacity
    )
    return (pivot_part[None], assembled[None])


def solution(mesh):
    return jax.shard_map(
        shards,
        mesh=mesh,
        in_specs=(P("front", "leaf", None), P("front", "leaf", None), P("front", "leaf")),
        out_specs=(P("front", "leaf", None), P("front", "leaf", None)),
        check_vma=False,
    )
```

```python
import functools
import jax
import jax.numpy as jnp
from jax import lax
from jax.experimental import pallas as pl
from jax.experimental.pallas import tpu as pltpu
from jax.sharding import PartitionSpec as P

PIV = 256
PR_DEV = 64
STRIP = 8
SUB = 32
PANEL = 128
CHUNK = 16
MESH = pl.DeviceIdType.MESH


highest = lax.Precision.HIGHEST


def factor_strip(a_ref, start, panel, strip, width):
    blocks = width // PANEL
    diag = a_ref[pl.ds(start, STRIP), pl.ds(pl.multiple_of(panel * PANEL, PANEL), PANEL)]
    c = {}
    for k in range(STRIP):
        lane = strip * STRIP + k
        column = jnp.broadcast_to(diag[:, lane:lane + 1], (STRIP, PANEL))
        for i in range(k, STRIP):
            c[i, k] = jnp.broadcast_to(column[i:i + 1, :], (STRIP, PANEL))
    body = [a_ref[pl.ds(start, STRIP), b * PANEL:(b + 1) * PANEL] for b in range(blocks)]
    body.append(diag)
    rows = [[jnp.broadcast_to(x[k:k + 1, :], (STRIP, PANEL)) for x in body] for k in range(STRIP)]
    for k in range(STRIP):
        inv = lax.rsqrt(c[k, k])
        rows[k] = [x * inv for x in rows[k]]
        for i in range(k + 1, STRIP):
            c[i, k] = c[i, k] * inv
        for i in range(k + 1, STRIP):
            for j in range(k + 1, i + 1):
                c[i, j] = c[i, j] - c[i, k] * c[j, k]
            rows[i] = [x - c[i, k] * y for x, y in zip(rows[i], rows[k])]
    sub = lax.broadcasted_iota(jnp.int32, (STRIP, PANEL), 0)
    lanes = lax.broadcasted_iota(jnp.int32, (STRIP, PANEL), 1)
    for b in range(blocks):
        out = rows[0][b]
        for k in range(1, STRIP):
            out = jnp.where(sub == k, rows[k][b], out)
        a_ref[pl.ds(start, STRIP), b * PANEL:(b + 1) * PANEL] = out
    return rows, sub, lanes


def one_hot_dot(picks, values):
    total = None
    for _ in range(3):
        piece = values.astype(jnp.bfloat16)
        values = values - piece.astype(jnp.float32)
        part = jnp.dot(picks, piece, preferred_element_type=jnp.float32)
        total = part if total is None else total + part
    return total


def front_kernel(
    x_ref, owner_ref, target_ref, pivot_ref, sum_ref, a_ref, update, select, dest_ref, high, low, own, in_l, in_r, out_l, out_r,
    rows_out, rows_in, dest_in, send_l, recv_l, send_r, recv_r, row_send, row_recv, dest_send, dest_recv,
):
    width = a_ref.shape[0]
    blocks = width // PANEL
    packed = (blocks + 1) // 2
    chunks = packed * PANEL // CHUNK
    per_panel = PANEL // CHUNK
    me, n = lax.axis_index("leaf"), lax.axis_size("leaf")
    has_left, has_right = me > 0, me < n - 1
    front, fronts = lax.axis_index("front"), lax.axis_size("front")
    slots, contrib_count = select.shape
    capacity = slots // fronts
    contrib_blocks = (width - PIV) // PANEL
    first_block = me * contrib_count // PANEL
    last_panel = (PIV + (me + 1) * contrib_count - 1) // PANEL
    peers = [lax.rem(front + d, fronts) for d in range(1, fronts)]

    barrier = pltpu.get_barrier_semaphore()

    @pl.when(has_left)
    def _():
        pl.semaphore_signal(barrier, inc=1, device_id={"leaf": me - 1}, device_id_type=MESH)

    @pl.when(has_right)
    def _():
        pl.semaphore_signal(barrier, inc=1, device_id={"leaf": me + 1}, device_id_type=MESH)

    rows_in[...] = jnp.zeros_like(rows_in)
    for peer in peers:
        pl.semaphore_signal(barrier, inc=1, device_id={"front": peer}, device_id_type=MESH)

    @pl.when(jnp.logical_not(has_left))
    def _():
        in_l[...] = jnp.zeros_like(in_l)

    @pl.when(jnp.logical_not(has_right))
    def _():
        in_r[...] = jnp.zeros_like(in_r)

    a_ref[...] = jnp.zeros_like(a_ref)
    update[...] = jnp.zeros_like(update)
    sum_ref[...] = jnp.zeros_like(sum_ref)
    high[...] = x_ref[...].astype(jnp.bfloat16)
    low[...] = (x_ref[...] - high[...].astype(jnp.float32)).astype(jnp.bfloat16)

    inner = jnp.logical_and(has_left, has_right)

    @pl.when(inner)
    def _():
        pl.semaphore_wait(barrier, 2 + fronts - 1)

    @pl.when(jnp.logical_not(inner))
    def _():
        pl.semaphore_wait(barrier, 1 + fronts - 1)

    def slots_of(g):
        return pl.ds(pl.multiple_of(g * capacity, STRIP), capacity)

    def dest_copy(to, src):
        return pltpu.make_async_remote_copy(
            src_ref=dest_ref.at[slots_of(to)], dst_ref=dest_in.at[slots_of(src)],
            send_sem=dest_send.at[to], recv_sem=dest_recv.at[src],
            device_id={"front": to}, device_id_type=MESH,
        )

    def row_copy(to, src, j):
        at = pl.ds(pl.multiple_of(j * PANEL, PANEL), PANEL)
        return pltpu.make_async_remote_copy(
            src_ref=rows_out.at[slots_of(to), at], dst_ref=rows_in.at[slots_of(src), at],
            send_sem=row_send.at[to, j], recv_sem=row_recv.at[src, j],
            device_id={"front": to}, device_id_type=MESH,
        )

    def send_rows():
        start = pl.multiple_of(PIV + me * contrib_count, STRIP)
        row = lax.broadcasted_iota(jnp.int32, (contrib_count, PANEL), 0) + me * contrib_count
        lane = lax.broadcasted_iota(jnp.int32, (contrib_count, PANEL), 1)

        def block(j, carry):
            at = pl.ds(pl.multiple_of(j * PANEL, PANEL), PANEL)
            rows = a_ref[pl.ds(start, contrib_count), pl.ds(pl.multiple_of(PIV + j * PANEL, PANEL), PANEL)]
            rows_out[:, at] = one_hot_dot(select[...], jnp.where(row <= lane + j * PANEL, rows, 0.0))
            for peer in peers:
                row_copy(peer, front, j).start()
            rows_in[slots_of(front), at] = rows_out[slots_of(front), at]
            return carry

        lax.fori_loop(first_block, contrib_blocks, block, 0)

    def prepare_slots():
        mine = jnp.broadcast_to(owner_ref[...].astype(jnp.float32), (contrib_count, PANEL))
        owner_row = mine.T[0:1, :]
        square = (contrib_count, contrib_count)
        before = lax.broadcasted_iota(jnp.int32, square, 0) < lax.broadcasted_iota(jnp.int32, square, 1)
        same = owner_ref[...].astype(jnp.float32) == owner_row
        rank = jnp.sum(jnp.where(same & before, 1.0, 0.0), axis=0, keepdims=True)
        slot_row = owner_row * capacity + rank
        chosen = lax.broadcasted_iota(jnp.int32, (slots, contrib_count), 0).astype(jnp.float32) == slot_row
        select[...] = jnp.where(chosen, 1.0, 0.0).astype(jnp.bfloat16)
        wanted = jnp.where(chosen, target_ref[...].astype(jnp.float32) + 1.0, 0.0)
        dest_ref[...] = jnp.broadcast_to(jnp.sum(wanted, axis=1, keepdims=True), dest_ref.shape)
        for peer in peers:
            dest_copy(peer, front).start()

    def rows_of(c):
        return pl.ds(pl.multiple_of(c * CHUNK, CHUNK), CHUNK)

    def to_right(src, c):
        return pltpu.make_async_remote_copy(
            src_ref=src.at[rows_of(c)], dst_ref=in_l.at[rows_of(c)],
            send_sem=send_r.at[c], recv_sem=recv_l.at[c],
            device_id={"leaf": me + 1}, device_id_type=MESH,
        )

    def to_left(src, c):
        return pltpu.make_async_remote_copy(
            src_ref=src.at[rows_of(c)], dst_ref=in_r.at[rows_of(c)],
            send_sem=send_l.at[c], recv_sem=recv_r.at[c],
            device_id={"leaf": me - 1}, device_id_type=MESH,
        )

    def from_left(c):
        @pl.when(has_left)
        def _():
            to_right(out_r, c).wait_recv()

            @pl.when(has_right)
            def _():
                out_r[rows_of(c), :] = own[rows_of(c), :] + in_l[rows_of(c), :]
                to_right(out_r, c).start()

    def from_right(c):
        @pl.when(has_right)
        def _():
            to_left(out_l, c).wait_recv()

            @pl.when(has_left)
            def _():
                out_l[rows_of(c), :] = own[rows_of(c), :] + in_r[rows_of(c), :]
                to_left(out_l, c).start()

    first_half = 2 * me < n

    def near(c):
        @pl.when(first_half)
        def _():
            from_left(c)

        @pl.when(jnp.logical_not(first_half))
        def _():
            from_right(c)

    def far(c):
        @pl.when(first_half)
        def _():
            from_right(c)

        @pl.when(jnp.logical_not(first_half))
        def _():
            from_left(c)

    def gram(panel, rows, at):
        cols = slice(panel * PANEL, (panel + 1) * PANEL)
        xt = x_ref[:, cols].T
        ht = xt.astype(jnp.bfloat16)
        lt = (xt - ht.astype(jnp.float32)).astype(jnp.bfloat16)
        right = slice(panel * PANEL, width)
        own[rows, at] = (
            jnp.dot(ht, high[:, right], preferred_element_type=jnp.float32)
            + jnp.dot(ht, low[:, right], preferred_element_type=jnp.float32)
            + jnp.dot(lt, high[:, right], preferred_element_type=jnp.float32)
        )

    def slot(k):
        if k <= per_panel:
            near(k)
            if k:
                far(k - 1)

    for q in range(packed):
        rows = slice(q * PANEL, (q + 1) * PANEL)
        gram(q, rows, slice(q * PANEL, width))
        if q:
            slot(2 * q - 2)
            gram(blocks - q, rows, slice(0, q * PANEL))

        @pl.when(jnp.logical_not(has_left))
        def _():
            for c in range(q * per_panel, (q + 1) * per_panel):
                to_right(own, c).start()

        @pl.when(jnp.logical_not(has_right))
        def _():
            for c in range(q * per_panel, (q + 1) * per_panel):
                to_left(own, c).start()

        if q:
            slot(2 * q - 1)
        else:
            prepare_slots()
    for k in range(2 * packed - 2, per_panel + 1):
        slot(k)

    def one_panel(panel, carry):
        base = pl.multiple_of(panel * PANEL, PANEL)
        folded = panel >= packed
        source = pl.ds(pl.multiple_of(jnp.where(folded, blocks - panel, panel) * PANEL, PANEL), PANEL)
        shift = jnp.where(folded, panel, 0)

        def total(j, carry):
            at = pl.ds(pl.multiple_of((j - shift) * PANEL, PANEL), PANEL)
            a_ref[pl.ds(base, PANEL), pl.ds(pl.multiple_of(j * PANEL, PANEL), PANEL)] = (
                own[source, at] + in_l[source, at] + in_r[source, at]
            ) - update[:, pl.ds(pl.multiple_of(j * PANEL, PANEL), PANEL)]
            return carry

        lax.fori_loop(panel, blocks, total, 0)

        @pl.when(panel > 0)
        def _():
            done = pl.ds(pl.multiple_of(base - PANEL, PANEL), PANEL)
            head = a_ref[done, pl.ds(base, PANEL)].T
            a_ref[pl.ds(base, PANEL), :] = a_ref[pl.ds(base, PANEL), :] - jnp.dot(
                head, a_ref[done, :], precision=lax.Precision.HIGH, preferred_element_type=jnp.float32
            )

        following = pl.multiple_of(jnp.minimum(panel + 1, blocks - 1) * PANEL, PANEL)
        batch = -(-(blocks - 1) // (PANEL // SUB)) * PANEL
        for group in range(PANEL // SUB):
            for part in range(SUB // CHUNK):
                c = (panel + 1) * per_panel + group * (SUB // CHUNK) + part

                @pl.when(c + 1 < chunks)
                def _():
                    near(c + 1)

                @pl.when(c < chunks)
                def _():
                    far(c)

            if group * batch < (blocks - 1) * PANEL:
                done = slice(group * batch, min((group + 1) * batch, (blocks - 1) * PANEL))
                head = a_ref[done, pl.ds(following, PANEL)]
                row = lax.broadcasted_iota(jnp.int32, head.shape, 0) + group * batch
                part = jnp.dot(
                    jnp.where(row < base, head, 0.0).T, a_ref[done, :],
                    precision=lax.Precision.HIGH, preferred_element_type=jnp.float32,
                )
                update[...] = update[...] + part if group else part
            for t in range(SUB // STRIP):
                strip = group * (SUB // STRIP) + t
                start = pl.multiple_of(base + strip * STRIP, STRIP)
                rows, sub, lanes = factor_strip(a_ref, start, panel, strip, width)
                for later in range(strip + 1, (group + 1) * (SUB // STRIP)):
                    below = pl.multiple_of(base + later * STRIP, STRIP)
                    picked = lanes == sub + later * STRIP
                    mult = [
                        jnp.sum(jnp.where(picked, rows[k][blocks], 0.0), axis=1, keepdims=True)
                        for k in range(STRIP)
                    ]
                    for b in range(blocks):
                        at = (pl.ds(below, STRIP), slice(b * PANEL, (b + 1) * PANEL))
                        terms = [mult[k] * rows[k][b] for k in range(STRIP)]
                        while len(terms) > 1:
                            terms = [x + y for x, y in zip(terms[::2], terms[1::2])]
                        a_ref[at] = a_ref[at] - terms[0]
            if group < PANEL // SUB - 1:
                done = pl.ds(pl.multiple_of(base + group * SUB, SUB), SUB)
                left = PANEL - (group + 1) * SUB
                head = a_ref[done, pl.ds(base, PANEL)].T[(group + 1) * SUB:, :]
                rest = pl.ds(pl.multiple_of(base + (group + 1) * SUB, SUB), left)
                a_ref[rest, :] = a_ref[rest, :] - jnp.dot(
                    head, a_ref[done, :], precision=lax.Precision.HIGH, preferred_element_type=jnp.float32
                )

        @pl.when(panel == last_panel)
        def _():
            send_rows()

        return carry

    lax.fori_loop(0, blocks, one_panel, 0)
    pivot_count = pivot_ref.shape[0]
    row = lax.broadcasted_iota(jnp.int32, (pivot_count, width), 0) + me * pivot_count
    pivot_ref[...] = jnp.where(
        row <= lax.broadcasted_iota(jnp.int32, (pivot_count, width), 1),
        a_ref[pl.ds(pl.multiple_of(me * pivot_count, STRIP), pivot_count), :],
        0.0,
    )
    dest_in[slots_of(front), :] = dest_ref[slots_of(front), :]
    for peer in peers:
        dest_copy(peer, peer).wait_recv()
    target = lax.broadcasted_iota(jnp.int32, (slots, PANEL), 1).astype(jnp.float32) + 1.0
    place = (dest_in[...] == target).astype(jnp.float32).T[:PR_DEV, :].astype(jnp.bfloat16)

    def arrived(j, carry):
        at = pl.ds(pl.multiple_of(j * PANEL, PANEL), PANEL)
        for peer in peers:
            row_copy(peer, peer, j).wait_recv()
        sum_ref[:, at] = one_hot_dot(place, rows_in[:, at])
        return carry

    lax.fori_loop(first_block, contrib_blocks, arrived, 0)

    for peer in peers:
        dest_copy(peer, peer).wait_send()

        def left(j, carry, peer=peer):
            row_copy(peer, peer, j).wait_send()
            return carry

        lax.fori_loop(first_block, contrib_blocks, left, 0)

    def finish(c, carry):
        @pl.when(has_right)
        def _():
            to_right(out_r, c).wait_send()

        @pl.when(has_left)
        def _():
            to_left(out_l, c).wait_send()

        return carry

    lax.fori_loop(0, chunks, finish, 0)


def front_factor(x, owners, targets, fronts, pivot_count, capacity):
    rows, width = x.shape
    packed = (width // PANEL + 1) // 2 * PANEL
    slots = fronts * capacity
    contrib_width = width - PIV
    sums = pltpu.VMEM((packed, width), jnp.float32)
    sems = pltpu.SemaphoreType.DMA((packed // CHUNK,))
    row_sems = pltpu.SemaphoreType.DMA((fronts, contrib_width // PANEL))
    dest_sems = pltpu.SemaphoreType.DMA((fronts,))
    return pl.pallas_call(
        front_kernel,
        out_shape=(
            jax.ShapeDtypeStruct((pivot_count, width), jnp.float32),
            jax.ShapeDtypeStruct((PR_DEV, contrib_width), jnp.float32),
        ),
        in_specs=[pl.BlockSpec(memory_space=pltpu.VMEM)] * 3,
        out_specs=[pl.BlockSpec(memory_space=pltpu.VMEM)] * 2,
        scratch_shapes=[pltpu.VMEM((width, width), jnp.float32), pltpu.VMEM((PANEL, width), jnp.float32)]
        + [pltpu.VMEM((slots, owners.shape[0]), jnp.bfloat16), pltpu.VMEM((slots, PANEL), jnp.float32)]
        + [pltpu.VMEM((rows, width), jnp.bfloat16)] * 2
        + [sums] * 5
        + [pltpu.VMEM((slots, contrib_width), jnp.float32)] * 2
        + [pltpu.VMEM((slots, PANEL), jnp.float32)]
        + [sems] * 4
        + [row_sems] * 2
        + [dest_sems] * 2,
        compiler_params=pltpu.CompilerParams(
            vmem_limit_bytes=48 * 1024 * 1024, collective_id=0, has_side_effects=True
        ),
        name="front_factor",
    )(x, owners, targets)


def shards(stacked, row_owner, dest_local):
    contrib_count = row_owner.shape[1]
    pivot_count = PIV // lax.axis_size("leaf")
    fronts = lax.axis_size("front")
    capacity = max(2, (2 * contrib_count + fronts - 1) // fronts)
    capacity = (capacity + STRIP - 1) // STRIP * STRIP
    pivot_part, assembled = front_factor(
        stacked[0], row_owner[0], dest_local, fronts, pivot_count, capacity
    )
    return (pivot_part[None], assembled[None])


def solution(mesh):
    return jax.shard_map(
        shards,
        mesh=mesh,
        in_specs=(P("front", "leaf", None), P("front", "leaf", None), P("front", "leaf")),
        out_specs=(P("front", "leaf", None), P("front", "leaf", None)),
        check_vma=False,
    )
```
